128 devices in a mesh: tm: 16 (over z_lo, x, core), op: 8 (over z_hi, y).
Axes of the slice: x: 4, y: 4, z: 4 (z_hi: 2, z_lo: 2; z = z_hi * 2 + z_lo), core: 2. Of those that a mesh axis runs over, the one named last changes fastest.
Arguments:
- perambs: float32 [16, 16, 2, 256, 256], P('tm'), may hold values from -0.25 to 0.25
- src_ops: float32 [8, 16, 2, 256, 256], P('op', 'tm'), may hold values from -0.25 to 0.25
- sink_ops: float32 [8, 16, 2, 256, 256], P('op', 'tm'), may hold values from -0.25 to 0.25
- pair_list: int32 [8, 4], P('op'), may hold values from 0 to 7
- pair_count: int32 [8], P('op'), may hold values from 1 to 4, as said below
Outputs:
- corr: float32 [8, 4, 16, 2, 16], P('op', None, 'tm')
The draws below stay inside these ranges and needn't reach their ends.
Inputs may be any that keep to these rules, and one draw needn't show every extreme that they name: The owner of operator a has pair_count[a] diagrams in slots 0 to pair_count[a] - 1; later slots hold no diagram. Some operator has all 4 slots filled in every draw.
All inputs are finite; a program needn't handle non-finite values.
Results may differ from the reference program's by a relative error of at most 0.0003.
Values sent between devices are 32-bit elements; how exact they have to be, the bound alone decides.
No kernel may reach another device: no remote copies, remote signals or barrier semaphores. Data moves between devices by JAX's collectives and lax.ppermute only.
A program may use at most 64 MiB of HBM per device.

```python
import jax
import jax.numpy as jnp
from jax import lax

ORDER = 256
SLOTS = 4
T_SIZE = 16
OPS = 8


def draw_pair_count(key, part):
    first, second = jax.random.split(jax.random.fold_in(key, 11))
    counts = jax.random.randint(first, (OPS,), 1, SLOTS + 1)
    fullest = jax.random.randint(second, (), 0, OPS)
    return jnp.where(jnp.arange(OPS) == fullest, SLOTS, counts).astype(jnp.int32)


def with_ends(entries, rng, least, high):
    index_at = [jax.random.randint(jax.random.fold_in(rng, axis), (), 0, length) for axis, length in enumerate(entries.shape)]
    main_axis = entries.shape.index(max(entries.shape))
    neighbour = index_at[:main_axis] + [(index_at[main_axis] + 1) % entries.shape[main_axis]] + index_at[main_axis + 1:]
    return entries.at[tuple(index_at)].set(least).at[tuple(neighbour)].set(high)


def steps_of(key, extent, cuts, low, largest):
    gain, own = 1.0, jax.random.fold_in(key, 6)
    for dim, blocks in cuts:
        steps = jnp.exp(jax.random.uniform(jax.random.fold_in(own, dim), (blocks,), jnp.float32, low / len(cuts), largest / len(cuts)))
        gain = gain * jnp.repeat(steps, extent[dim] // blocks).reshape([-1 if axis == dim else 1 for axis in range(len(extent))])
    return gain


def noise(rng, dims, spread, most, pieces=(), kind=jnp.bfloat16):
    array = spread * jax.random.normal(rng, dims, jnp.float32)
    if pieces:
        array = array * steps_of(rng, dims, pieces, -0.22, 0.18)
    return jnp.clip(array, -most, most).astype(kind)


def setup_inputs(seed: int = 0) -> dict:
    key_of = jax.random.split(jax.random.key(seed), 6)
    perambs = noise(key_of[0], (T_SIZE, T_SIZE, 2, ORDER, ORDER), (2 * ORDER) ** -0.5, 0.25, ((0, 16),), jnp.float32)
    src_ops = noise(key_of[1], (OPS, T_SIZE, 2, ORDER, ORDER), (2 * ORDER) ** -0.5, 0.25, ((0, 8), (1, 16)), jnp.float32)
    sink_ops = noise(key_of[2], (OPS, T_SIZE, 2, ORDER, ORDER), (2 * ORDER) ** -0.5, 0.25, ((0, 8), (1, 16)), jnp.float32)
    pair_list = with_ends(jax.random.randint(key_of[3], (OPS, SLOTS), 0, OPS), jax.random.fold_in(key_of[3], 1), 0, OPS - 1).astype(jnp.int32)
    pair_count = draw_pair_count(jax.random.fold_in(key_of[5], 71), 0)
    return dict(perambs=perambs, src_ops=src_ops, sink_ops=sink_ops, pair_list=pair_list, pair_count=pair_count)


highest = lax.Precision.HIGHEST


def complex_product(left_re, left_im, right_re, right_im):
    real_part = jnp.matmul(left_re, right_re, precision=highest) - jnp.matmul(left_im, right_im, precision=highest)
    imag_part = jnp.matmul(left_re, right_im, precision=highest) + jnp.matmul(left_im, right_re, precision=highest)
    return real_part, imag_part


def reference(perambs, src_ops, sink_ops, pair_list, pair_count):
    slot_index = jnp.arange(SLOTS).astype(jnp.int32)

    def one_owner(owner):
        source = src_ops[owner]
        listing = pair_list[owner]
        live = (slot_index < pair_count[owner]).astype(jnp.float32)

        def one_sink(sink):
            peramb = perambs[sink]
            chosen = jnp.take(sink_ops[:, sink], listing, axis=0)
            half_re, half_im = complex_product(peramb[:, 0], peramb[:, 1], source[:, 0], source[:, 1])
            prod_re, prod_im = complex_product(half_re, half_im, jnp.swapaxes(peramb[:, 0], 1, 2), -jnp.swapaxes(peramb[:, 1], 1, 2))
            pair_re, pair_im = complex_product(prod_re[:, None], prod_im[:, None], chosen[None, :, 0], chosen[None, :, 1])
            swap_re = jnp.swapaxes(pair_re, 2, 3)
            swap_im = jnp.swapaxes(pair_im, 2, 3)
            trace_re = jnp.sum(pair_re * swap_re, axis=(2, 3)) - jnp.sum(pair_im * swap_im, axis=(2, 3))
            trace_im = 2.0 * jnp.sum(pair_re * swap_im, axis=(2, 3))
            values = jnp.stack([trace_re, trace_im], axis=0)
            values = jnp.transpose(values, (2, 0, 1))
            return values * live[:, None, None]

        table = lax.map(one_sink, jnp.arange(T_SIZE).astype(jnp.int32))
        return jnp.transpose(table, (1, 0, 2, 3))

    return lax.map(one_owner, jnp.arange(OPS).astype(jnp.int32))
```

```python
import functools
import itertools

import jax
import jax.numpy as jnp
from jax import lax
from jax.experimental import pallas as pl
from jax.experimental.pallas import tpu as pltpu
from jax.sharding import PartitionSpec as P

AXES = ("tm", "op")
N = 256
SLOTS = 4
TIMES = 16
HALF = jnp.bfloat16
FULL = jnp.float32
NN = (((1,), (0,)), ((), ()))
NT = (((1,), (1,)), ((), ()))


def moves(dx=0, dy=0, core=0, z_lo=0, z_hi=0):
    def index(zl, x, c, zh, y):
        return ((zl * 4 + x % 4) * 2 + c) * 8 + zh * 4 + y % 4

    return [
        (index(zl, x, c, zh, y), index(zl ^ z_lo, x + dx, c ^ core, zh ^ z_hi, y + dy))
        for zl, x, c, zh, y in itertools.product(range(2), range(4), range(2), range(2), range(4))
    ]


def send(value, **step):
    return lax.ppermute(value, AXES, moves(**step))


def split(x):
    high = x.astype(HALF)
    return high, (x - high.astype(FULL)).astype(HALF)


def left(x):
    high, low = split(x)
    return jnp.concatenate([high, low, high], axis=1)


def right(x):
    high, low = split(x)
    return jnp.concatenate([high, high, low], axis=0)


def right_rows(x):
    high, low = split(x)
    return jnp.concatenate([high, high, low], axis=1)


def product(a, b, dims):
    return lax.dot_general(a, b, dims, preferred_element_type=FULL)


def x_kernel(times, count, *refs):
    peramb, source, out = refs[:count], refs[count : 2 * count], refs[-1]
    for j in range(count):
        pr, pi = peramb[j][0, 0], peramb[j][0, 1]
        ar, ai = source[j][0], source[j][1]
        k1 = product(left(ar + ai), right_rows(pr), NT)
        k2 = product(left(ar), right_rows(-pi - pr), NT)
        k3 = product(left(ai), right_rows(pr - pi), NT)
        hr, hi = k1 - k3, k1 + k2
        k1 = product(left(pr + pi), right(hr), NN)
        k2 = product(left(pr), right(hi - hr), NN)
        k3 = product(left(pi), right(hr + hi), NN)
        out[j, 0] = k1 - k3
        out[j, 1] = k1 + k2


def make_x(times, peramb, sources):
    count = len(sources)

    def body(times, *refs):
        x_kernel(times, count, *refs)

    def at(j):
        return pl.BlockSpec((1, 2, N, N), lambda g, times: (times[j], 0, 0, 0))

    whole = pl.BlockSpec((2, N, N), lambda g, times: (0, 0, 0))
    return pl.pallas_call(
        body,
        out_shape=jax.ShapeDtypeStruct((count, 2, N, N), FULL),
        grid_spec=pltpu.PrefetchScalarGridSpec(
            num_scalar_prefetch=1,
            grid=(1,),
            in_specs=[at(j) for j in range(count)] + [whole] * count,
            out_specs=pl.BlockSpec((count, 2, N, N), lambda g, times: (0, 0, 0, 0)),
        ),
        compiler_params=pltpu.CompilerParams(vmem_limit_bytes=40 << 20),
        cost_estimate=pl.CostEstimate(
            flops=count * 18 * 2 * N**3, bytes_accessed=count * 6 * N * N * 4, transcendentals=0
        ),
        name="make_x",
    )(times, *([peramb] * count), *sources)


def trace_parts(zr, zi):
    zrt, zit = zr.T, zi.T
    re = (zr * zrt - zi * zit).reshape(32, 8, N).sum(0)
    im = (zr * zit).reshape(32, 8, N).sum(0)
    return re[:, :128] + re[:, 128:], 2.0 * (im[:, :128] + im[:, 128:])


def z_kernel(groups, places, count_ref, times, *refs):
    total = sum(groups)
    xs = refs[: len(groups)]
    whole, parts = refs[len(groups) : len(groups) + 6], refs[len(groups) + 6 : len(groups) + 10]
    out, sinks, x_all, ready, acc, sems, x_sems = refs[len(groups) + 10 :]
    step = pl.program_id(0)

    def s_copies():
        copies = [pltpu.make_async_copy(ref, sinks.at[k], sems.at[k]) for k, ref in enumerate(whole)]
        for k, ref in enumerate(parts):
            copies.append(pltpu.make_async_copy(ref, sinks.at[6 + k // 2, k % 2], sems.at[6 + k]))
        return copies

    def x_copies():
        copies, start = [], 0
        for k, size in enumerate(groups):
            copies.append(pltpu.make_async_copy(xs[k], x_all.at[pl.ds(start, size)], x_sems.at[k]))
            start += size
        return copies

    @pl.when(step == 0)
    def _():
        for copy in s_copies() + x_copies():
            copy.start()
        for copy in s_copies():
            copy.wait()
        for s in range(SLOTS):
            sr, si = sinks[places[s], 0], sinks[places[s], 1]
            ready[s, 0] = right(sr)
            ready[s, 1] = right(si - sr)
            ready[s, 2] = right(si + sr)
        for copy in x_copies():
            copy.wait()

    rows = 2 * N
    xr = x_all[pl.ds(2 * step, 2), 0].reshape(rows, N)
    xi = x_all[pl.ds(2 * step, 2), 1].reshape(rows, N)
    x0, x1, x2 = left(xr + xi), left(xr), left(xi)
    for s in range(SLOTS):
        k1 = product(x0, ready[s, 0], NN)
        k2 = product(x1, ready[s, 1], NN)
        k3 = product(x2, ready[s, 2], NN)
        zr, zi = k1 - k3, k1 + k2
        for j in range(2):
            re, im = trace_parts(zr[j * N : (j + 1) * N], zi[j * N : (j + 1) * N])
            at = times[2 * step + j]
            acc[s, 0, at] = re
            acc[s, 1, at] = im

    @pl.when(step == pl.num_programs(0) - 1)
    def _():
        slot = lax.broadcasted_iota(jnp.int32, (SLOTS, 2, TIMES), 0)
        out[...] = jnp.where(slot < count_ref[0], acc[...].sum((3, 4)), 0.0)


def make_z(places, count, times, xs, whole, parts):
    groups = tuple(x.shape[0] for x in xs)
    total = sum(groups)
    anywhere = pl.BlockSpec(memory_space=pl.ANY)
    return pl.pallas_call(
        functools.partial(z_kernel, groups),
        out_shape=jax.ShapeDtypeStruct((SLOTS, 2, TIMES), FULL),
        grid_spec=pltpu.PrefetchScalarGridSpec(
            num_scalar_prefetch=3,
            grid=(total // 2,),
            in_specs=[anywhere] * (len(xs) + len(whole) + len(parts)),
            out_specs=pl.BlockSpec((SLOTS, 2, TIMES), lambda g, *_: (0, 0, 0)),
            scratch_shapes=[
                pltpu.VMEM((8, 2, N, N), FULL),
                pltpu.VMEM((total, 2, N, N), FULL),
                pltpu.VMEM((SLOTS, 3, 3 * N, N), HALF),
                pltpu.VMEM((SLOTS, 2, TIMES, 8, 128), FULL),
                pltpu.SemaphoreType.DMA((10,)),
                pltpu.SemaphoreType.DMA((len(xs),)),
            ],
        ),
        compiler_params=pltpu.CompilerParams(
            vmem_limit_bytes=40 << 20, dimension_semantics=("arbitrary",)
        ),
        cost_estimate=pl.CostEstimate(
            flops=total * SLOTS * 9 * 2 * N**3, bytes_accessed=16 << 20, transcendentals=0
        ),
        name="make_z",
    )(places, count, times, *xs, *whole, *parts)


def body(perambs, src_ops, sink_ops, pair_list, pair_count):
    peramb = perambs[0]
    a_own = src_ops[0, 0]
    s_own = sink_ops[0, 0]
    tm, op = lax.axis_index("tm"), lax.axis_index("op")
    x, y = (tm // 2) % 4, op % 4

    s_up = send(s_own, dy=1)
    s_down = send(s_own, dy=-1)
    s_far = send(s_own, z_hi=1)
    a_sib = send(a_own, core=1)
    a_up = send(a_own, dx=1)
    a_down = send(a_own, dx=-1)
    a_far = send(a_own, z_lo=1)
    s_far_up = send(s_far, dy=1)
    s_far_down = send(s_far, dy=-1)
    s_two = (send(s_up[0], dy=1), send(s_down[1], dy=-1))
    a_two = send(a_own, dx=2)
    s_far_two = (send(s_far_up[0], dy=1), send(s_far_down[1], dy=-1))
    a_far_up = send(a_far, dx=1)
    a_far_down = send(a_far, dx=-1)
    a_far_two = send(a_far, dx=2)

    blocks = [a_own, a_up, a_down, a_two, a_far, a_far_up, a_far_down, a_far_two]
    steps = [(0, 0), (0, -1), (0, 1), (0, 2), (1, 0), (1, -1), (1, 1), (1, 2)]
    xs, order = [], []
    for block, (plane, step) in zip(blocks, steps):
        there = a_sib if block is a_own else send(block, core=1)
        mine = (((tm // 8) ^ plane) * 4 + (x + step) % 4) * 2 + tm % 2
        times = jnp.stack([mine, mine ^ 1]).astype(jnp.int32)
        order.append(times)
        xs.append(make_x(times, peramb, [block, there]))

    b = pair_list[0]
    turn = (b - y) % 4
    near = jnp.where(turn == 0, 0, jnp.where(turn == 3, 1, jnp.where(turn == 1, 2, 6)))
    other = jnp.where(turn == 2, 7, near + 3)
    places = jnp.where((b // 4) == (op // 4), near, other).astype(jnp.int32)
    whole = [s_own, s_up, s_down, s_far, s_far_up, s_far_down]
    table = make_z(
        places, pair_count, jnp.concatenate(order), xs, whole, [*s_two, *s_far_two]
    )
    return table[None, :, None]


def solution(mesh):
    placed = (
        P("tm", None, None, None, None),
        P("op", "tm", None, None, None),
        P("op", "tm", None, None, None),
        P("op", None),
        P("op"),
    )
    return jax.shard_map(
        body, mesh=mesh, in_specs=placed, out_specs=P("op", None, "tm", None, None), check_vma=False
    )
```

```python
import functools
import itertools

import jax
import jax.numpy as jnp
from jax import lax
from jax.experimental import pallas as pl
from jax.experimental.pallas import tpu as pltpu
from jax.sharding import PartitionSpec as P

AXES = ("tm", "op")
N = 256
SLOTS = 4
NEAR = 5
TIMES = 16
HALF = jnp.bfloat16
FULL = jnp.float32
NN = (((1,), (0,)), ((), ()))
NT = (((1,), (1,)), ((), ()))


def moves(dx=0, dy=0, core=0, z_lo=0, z_hi=0):
    def index(zl, x, c, zh, y):
        return ((zl * 4 + x % 4) * 2 + c) * 8 + zh * 4 + y % 4

    return [
        (index(zl, x, c, zh, y), index(zl ^ z_lo, x + dx, c ^ core, zh ^ z_hi, y + dy))
        for zl, x, c, zh, y in itertools.product(range(2), range(4), range(2), range(2), range(4))
    ]


def send(value, **step):
    return lax.ppermute(value, AXES, moves(**step))


def split(x):
    high = x.astype(HALF)
    return high, (x - high.astype(FULL)).astype(HALF)


def left(x):
    high, low = split(x)
    return jnp.concatenate([high, low, high], axis=1)


def right(x):
    high, low = split(x)
    return jnp.concatenate([high, high, low], axis=0)


def right_rows(x):
    high, low = split(x)
    return jnp.concatenate([high, high, low], axis=1)


def product(a, b, dims):
    return lax.dot_general(a, b, dims, preferred_element_type=FULL)


def x_kernel(count, *refs):
    peramb, source, out = refs[:count], refs[count : 2 * count], refs[-1]
    for j in range(count):
        pr, pi = peramb[j][0, 0], peramb[j][0, 1]
        ar, ai = source[j][0], source[j][1]
        k1 = product(left(ar + ai), right_rows(pr), NT)
        k2 = product(left(ar), right_rows(-pi - pr), NT)
        k3 = product(left(ai), right_rows(pr - pi), NT)
        hr, hi = k1 - k3, k1 + k2
        k1 = product(left(pr + pi), right(hr), NN)
        k2 = product(left(pr), right(hi - hr), NN)
        k3 = product(left(pi), right(hr + hi), NN)
        out[j, 0] = k1 - k3
        out[j, 1] = k1 + k2


def make_x(times, peramb, sources):
    count = len(sources)

    def body(times, *refs):
        x_kernel(count, *refs)

    def at(j):
        return pl.BlockSpec((1, 2, N, N), lambda g, times: (times[j], 0, 0, 0))

    whole = pl.BlockSpec((2, N, N), lambda g, times: (0, 0, 0))
    return pl.pallas_call(
        body,
        out_shape=jax.ShapeDtypeStruct((count, 2, N, N), FULL),
        grid_spec=pltpu.PrefetchScalarGridSpec(
            num_scalar_prefetch=1,
            grid=(1,),
            in_specs=[at(j) for j in range(count)] + [whole] * count,
            out_specs=pl.BlockSpec((count, 2, N, N), lambda g, times: (0, 0, 0, 0)),
        ),
        compiler_params=pltpu.CompilerParams(vmem_limit_bytes=20 << 20),
        cost_estimate=pl.CostEstimate(
            flops=count * 18 * 2 * N**3, bytes_accessed=count * 6 * N * N * 4, transcendentals=0
        ),
        name="make_x",
    )(times, *([peramb] * count), *sources)


def trace_parts(zr, zi):
    zrt, zit = zr.T, zi.T
    re = (zr * zrt - zi * zit).reshape(32, 8, N).sum(0)
    im = (zr * zit).reshape(32, 8, N).sum(0)
    return re[:, :128] + re[:, 128:], 2.0 * (im[:, :128] + im[:, 128:])


def z_kernel(groups, places, count_ref, times, before, *refs):
    xs = refs[: len(groups)]
    blocks = refs[len(groups) : len(groups) + 8]
    out, sinks, x_all, ready, acc, sems, x_sems = refs[len(groups) + 8 :]
    step = pl.program_id(0)

    def s_copies():
        return [pltpu.make_async_copy(ref, sinks.at[k], sems.at[k]) for k, ref in enumerate(blocks)]

    def x_copies():
        copies, start = [], 0
        for k, size in enumerate(groups):
            copies.append(pltpu.make_async_copy(xs[k], x_all.at[pl.ds(start, size)], x_sems.at[k]))
            start += size
        return copies

    @pl.when(step == 0)
    def _():
        acc[...] = jnp.zeros_like(acc)
        for copy in s_copies() + x_copies():
            copy.start()
        for copy in s_copies():
            copy.wait()
        for s in range(SLOTS):
            sr, si = sinks[places[s], 0], sinks[places[s], 1]
            ready[s, 0] = right(sr)
            ready[s, 1] = right(si - sr)
            ready[s, 2] = right(si + sr)
        for copy in x_copies():
            copy.wait()

    rows = 2 * N
    xr = x_all[pl.ds(2 * step, 2), 0].reshape(rows, N)
    xi = x_all[pl.ds(2 * step, 2), 1].reshape(rows, N)
    x0, x1, x2 = left(xr + xi), left(xr), left(xi)
    for s in range(SLOTS):
        k1 = product(x0, ready[s, 0], NN)
        k2 = product(x1, ready[s, 1], NN)
        k3 = product(x2, ready[s, 2], NN)
        zr, zi = k1 - k3, k1 + k2
        for j in range(2):
            re, im = trace_parts(zr[j * N : (j + 1) * N], zi[j * N : (j + 1) * N])
            at = times[2 * step + j]
            acc[s, 0, at] = re
            acc[s, 1, at] = im

    @pl.when(step == pl.num_programs(0) - 1)
    def _():
        slot = lax.broadcasted_iota(jnp.int32, (SLOTS, 2, TIMES), 0)
        out[...] = before[...] + jnp.where(slot < count_ref[0], acc[...].sum((3, 4)), 0.0)


def make_z(places, count, times, before, xs, blocks):
    groups = tuple(x.shape[0] for x in xs)
    total = sum(groups)
    anywhere = pl.BlockSpec(memory_space=pl.ANY)
    table = pl.BlockSpec((SLOTS, 2, TIMES), lambda g, *_: (0, 0, 0))
    return pl.pallas_call(
        functools.partial(z_kernel, groups),
        out_shape=jax.ShapeDtypeStruct((SLOTS, 2, TIMES), FULL),
        grid_spec=pltpu.PrefetchScalarGridSpec(
            num_scalar_prefetch=3,
            grid=(total // 2,),
            in_specs=[table] + [anywhere] * (len(xs) + 8),
            out_specs=table,
            scratch_shapes=[
                pltpu.VMEM((8, 2, N, N), FULL),
                pltpu.VMEM((total, 2, N, N), FULL),
                pltpu.VMEM((SLOTS, 3, 3 * N, N), HALF),
                pltpu.VMEM((SLOTS, 2, TIMES, 8, 128), FULL),
                pltpu.SemaphoreType.DMA((8,)),
                pltpu.SemaphoreType.DMA((len(xs),)),
            ],
        ),
        compiler_params=pltpu.CompilerParams(
            vmem_limit_bytes=20 << 20, dimension_semantics=("arbitrary",)
        ),
        cost_estimate=pl.CostEstimate(
            flops=total * SLOTS * 9 * 2 * N**3, bytes_accessed=16 << 20, transcendentals=0
        ),
        name="make_z",
    )(places, count, times, before, *xs, *blocks)


def body(perambs, src_ops, sink_ops, pair_list, pair_count):
    peramb = perambs[0]
    a_own = src_ops[0, 0]
    s_own = sink_ops[0, 0]
    tm, op = lax.axis_index("tm"), lax.axis_index("op")
    x, y = (tm // 2) % 4, op % 4

    tie = lax.optimization_barrier
    s_up = send(s_own, dy=1)
    s_down = send(s_own, dy=-1)
    s_far = send(s_own, z_hi=1)
    a_up = send(a_own, dx=1)
    a_down = send(a_own, dx=-1)
    s_up, s_down, s_far, a_up, a_down, a_next = tie((s_up, s_down, s_far, a_up, a_down, a_own))
    s_far_down = send(s_far, dy=-1)
    s_far_up = send(s_far, dy=1)
    s_two = send(s_up, dy=1)
    a_far = send(a_next, z_lo=1)
    a_two = send(a_next, dx=2)
    s_far_down, a_far, a_next = tie((s_far_down, a_far, a_next))
    s_far_two = send(s_far_down, dy=-1)
    beside = [send(a, core=1) for a in (a_next, a_up, a_down)]
    a_two, s_two, s_far_up, beside = tie((a_two, s_two, s_far_up, beside))
    beside += [send(a, core=1) for a in (a_two, a_far)]
    a_far_up = send(a_far, dx=1)
    a_far_down = send(a_far, dx=-1)
    a_far_two = send(a_far, dx=2)

    def times_of(plane, step, other):
        mine = (((tm // 8) ^ plane) * 4 + (x + step) % 4) * 2 + tm % 2
        return mine ^ other

    def pair(first, second):
        (a, *at), (b, *bt) = first, second
        times = jnp.stack([times_of(*at), times_of(*bt)]).astype(jnp.int32)
        return make_x(times, peramb, [a, b]), times

    b = pair_list[0]
    places = ((b - y) % 4 + 4 * (b // 4 != op // 4)).astype(jnp.int32)
    sinks = [s_own, s_down, s_two, s_up, s_far, s_far_down, s_far_two, s_far_up]
    early = [(a_own, 0, 0), (a_up, 0, -1), (a_down, 0, 1), (a_two, 0, 2), (a_far, 1, 0)]
    done = [pair((a, *at, 0), (there, *at, 1)) for (a, *at), there in zip(early[:NEAR], beside)]
    table = jnp.zeros((SLOTS, 2, TIMES), FULL)
    table = make_z(places, pair_count, jnp.concatenate([t for _, t in done]), table, [v for v, _ in done], sinks)
    table, a_far_up, a_far_down, a_far_two = tie((table, a_far_up, a_far_down, a_far_two))
    done = [pair((a, *at, 0), (there, *at, 1)) for (a, *at), there in zip(early[NEAR:], beside[NEAR:])]
    late = [(a_far_up, 1, -1), (a_far_down, 1, 1), (a_far_two, 1, 2)]
    there = [send(a, core=1) for a, *_ in late]
    done.append(pair((a_far_up, 1, -1, 0), (a_far_down, 1, 1, 0)))
    done.append(pair((a_far_two, 1, 2, 0), (there[0], 1, -1, 1)))
    done.append(pair((there[1], 1, 1, 1), (there[2], 1, 2, 1)))
    table = make_z(places, pair_count, jnp.concatenate([t for _, t in done]), table, [v for v, _ in done], sinks)
    return table[None, :, None]


def solution(mesh):
    placed = (
        P("tm", None, None, None, None),
        P("op", "tm", None, None, None),
        P("op", "tm", None, None, None),
        P("op", None),
        P("op"),
    )
    return jax.shard_map(
        body, mesh=mesh, in_specs=placed, out_specs=P("op", None, "tm", None, None), check_vma=False
    )
```

```python
import itertools

import jax
import jax.numpy as jnp
from jax import lax
from jax.experimental import pallas as pl
from jax.experimental.pallas import tpu as pltpu
from jax.sharding import PartitionSpec as P

AXES = ("tm", "op")
N = 256
SLOTS = 4
TIMES = 16
HALF = jnp.bfloat16
FULL = jnp.float32
NN = (((1,), (0,)), ((), ()))
NT = (((1,), (1,)), ((), ()))


def moves(dx=0, dy=0, core=0, z_lo=0, z_hi=0):
    def index(zl, x, c, zh, y):
        return ((zl * 4 + x % 4) * 2 + c) * 8 + zh * 4 + y % 4

    return [
        (index(zl, x, c, zh, y), index(zl ^ z_lo, x + dx, c ^ core, zh ^ z_hi, y + dy))
        for zl, x, c, zh, y in itertools.product(range(2), range(4), range(2), range(2), range(4))
    ]


def send(value, **step):
    return lax.ppermute(value, AXES, moves(**step))


def split(x):
    high = x.astype(HALF)
    return high, (x - high.astype(FULL)).astype(HALF)


def left(x):
    high, low = split(x)
    return jnp.concatenate([high, low, high], axis=1)


def right(x):
    high, low = split(x)
    return jnp.concatenate([high, high, low], axis=0)


def product(a, b, dims):
    return lax.dot_general(a, b, dims, preferred_element_type=FULL)


def x_of(peramb, source):
    pr, pi = peramb
    ar, ai = source
    (prh, prl), (pih, pil), (psh, psl), (pdh, pdl) = map(split, (pr, pi, pr + pi, pr - pi))

    def down(high, low):
        return jnp.concatenate([high, high, low], axis=1)

    def along(high, low):
        return jnp.concatenate([high, low, high], axis=1)

    k1 = product(left(ar + ai), down(prh, prl), NT)
    k2 = product(left(ar), down(psh, psl), NT)
    k3 = product(left(ai), down(pdh, pdl), NT)
    hr, hi = k1 - k3, k1 - k2
    k1 = product(along(psh, psl), right(hr), NN)
    k2 = product(along(prh, prl), right(hi - hr), NN)
    k3 = product(along(pih, pil), right(hr + hi), NN)
    return k1 - k3, k1 + k2


def trace_parts(zr, zi):
    zrt, zit = zr.T, zi.T
    re = (zr * zrt - zi * zit).reshape(32, 8, N).sum(0)
    im = (zr * zit).reshape(32, 8, N).sum(0)
    return re[:, :128] + re[:, 128:], 2.0 * (im[:, :128] + im[:, 128:])


def traces(xr, xi, ready, acc, times, step):
    x0, x1, x2 = left(xr + xi), left(xr), left(xi)
    for s in range(SLOTS):
        k1 = product(x0, ready[s, 0], NN)
        k2 = product(x1, ready[s, 1], NN)
        k3 = product(x2, ready[s, 2], NN)
        zr, zi = k1 - k3, k1 + k2
        for j in range(2):
            re, im = trace_parts(zr[j * N : (j + 1) * N], zi[j * N : (j + 1) * N])
            at = times[2 * step + j]
            acc[s, 0, at] = re
            acc[s, 1, at] = im


def prepare(sinks, ready):
    for s in range(SLOTS):
        sr, si = sinks[s, 0], sinks[s, 1]
        ready[s, 0] = right(sr)
        ready[s, 1] = right(si - sr)
        ready[s, 2] = right(si + sr)


def fetch_sinks(places, refs, sinks, sems):
    for s in range(SLOTS):
        for k, ref in enumerate(refs):

            @pl.when(places[s] == k)
            def _():
                pltpu.make_async_copy(ref, sinks.at[s], sems.at[s]).start()


def both_steps(places, count, times, before, peramb, sources, blocks):
    total = len(sources)

    def kernel(places, count_ref, times, before, p_hbm, *refs):
        sources, blocks, out = refs[:total], refs[total : total + 8], refs[total + 8]
        p_all, a_all, sinks, ready, acc, p_sems, a_sems, s_sems = refs[total + 9 :]
        step = pl.program_id(0)

        @pl.when(step == 0)
        def _():
            for k in range(total):
                pltpu.make_async_copy(p_hbm.at[times[k]], p_all.at[k], p_sems.at[k]).start()
                pltpu.make_async_copy(sources[k], a_all.at[k], a_sems.at[k]).start()
                if k == 0:
                    fetch_sinks(places, blocks, sinks, s_sems)
            acc[...] = jnp.zeros_like(acc)
            for s in range(SLOTS):
                pltpu.make_async_copy(blocks[0], sinks.at[s], s_sems.at[s]).wait()
            prepare(sinks, ready)

        xs = []
        for j in range(2):
            k = 2 * step + j
            pltpu.make_async_copy(p_hbm.at[0], p_all.at[k], p_sems.at[k]).wait()
            pltpu.make_async_copy(sources[0], a_all.at[k], a_sems.at[k]).wait()
        for j in range(2):
            k = 2 * step + j
            xs.append(x_of((p_all[k, 0], p_all[k, 1]), (a_all[k, 0], a_all[k, 1])))
        xr, xi = (jnp.concatenate([xs[0][part], xs[1][part]], axis=0) for part in range(2))
        traces(xr, xi, ready, acc, times, step)

        @pl.when(step == pl.num_programs(0) - 1)
        def _():
            slot = lax.broadcasted_iota(jnp.int32, (SLOTS, 2, TIMES), 0)
            out[...] = before[...] + jnp.where(slot < count_ref[0], acc[...].sum((3, 4)), 0.0)

    hbm = pl.BlockSpec(memory_space=pltpu.HBM)
    table = pl.BlockSpec((SLOTS, 2, TIMES), lambda g, *_: (0, 0, 0))
    return pl.pallas_call(
        kernel,
        out_shape=jax.ShapeDtypeStruct((SLOTS, 2, TIMES), FULL),
        grid_spec=pltpu.PrefetchScalarGridSpec(
            num_scalar_prefetch=3,
            grid=(total // 2,),
            in_specs=[table] + [hbm] * (1 + total + 8),
            out_specs=table,
            scratch_shapes=[
                pltpu.VMEM((total, 2, N, N), FULL),
                pltpu.VMEM((total, 2, N, N), FULL),
                pltpu.VMEM((SLOTS, 2, N, N), FULL),
                pltpu.VMEM((SLOTS, 3, 3 * N, N), HALF),
                pltpu.VMEM((SLOTS, 2, TIMES, 8, 128), FULL),
                pltpu.SemaphoreType.DMA((total,)),
                pltpu.SemaphoreType.DMA((total,)),
                pltpu.SemaphoreType.DMA((SLOTS,)),
            ],
        ),
        compiler_params=pltpu.CompilerParams(
            vmem_limit_bytes=58 << 20, dimension_semantics=("arbitrary",)
        ),
        cost_estimate=pl.CostEstimate(
            flops=total * (18 + SLOTS * 9) * 2 * N**3, bytes_accessed=16 << 20, transcendentals=0
        ),
        name="both_steps",
    )(places, count, times, before, peramb, *sources, *blocks)


def body(perambs, src_ops, sink_ops, pair_list, pair_count):
    peramb = perambs[0]
    a_own = src_ops[0, 0]
    s_own = sink_ops[0, 0]
    tm, op = lax.axis_index("tm"), lax.axis_index("op")
    x, y = (tm // 2) % 4, op % 4

    tie = lax.optimization_barrier
    s_up = send(s_own, dy=1)
    s_down = send(s_own, dy=-1)
    s_far = send(s_own, z_hi=1)
    a_up = send(a_own, dx=1)
    a_down = send(a_own, dx=-1)
    def times_of(steps):
        return jnp.stack(
            [
                (((tm // 8) ^ plane) * 4 + (x + step) % 4) * 2 + (tm % 2 ^ other)
                for plane, step in steps
                for other in range(2)
            ]
        ).astype(jnp.int32)

    b = pair_list[0]
    scalars = (
        ((b - y) % 4 + 4 * (b // 4 != op // 4)).astype(jnp.int32),
        times_of([(0, 0), (0, -1), (0, 1), (0, 2), (1, 0)]),
        times_of([(1, -1), (1, 1), (1, 2)]),
        jnp.zeros((SLOTS, 2, TIMES), FULL),
    )
    s_up, s_down, s_far, a_up, a_down, a_next, scalars = tie(
        (s_up, s_down, s_far, a_up, a_down, a_own, scalars)
    )
    places, first_times, last_times, table = scalars
    s_far_down = send(s_far, dy=-1)
    s_far_up = send(s_far, dy=1)
    s_two = send(s_up, dy=1)
    a_far = send(a_next, z_lo=1)
    a_two = send(a_next, dx=2)
    s_far_down, a_far, a_next = tie((s_far_down, a_far, a_next))
    s_far_two = send(s_far_down, dy=-1)
    beside = [send(a, core=1) for a in (a_next, a_up, a_down)]
    a_two, s_two, s_far_up, s_far_two, beside = tie((a_two, s_two, s_far_up, s_far_two, beside))
    beside += [send(a, core=1) for a in (a_two, a_far)]
    a_far_up = send(a_far, dx=1)
    a_far_down = send(a_far, dx=-1)
    a_far_two = send(a_far, dx=2)

    sinks = [s_own, s_down, s_two, s_up, s_far, s_far_down, s_far_two, s_far_up]
    first = [m for a, there in zip((a_own, a_up, a_down, a_two, a_far), beside) for m in (a, there)]
    table = both_steps(places, pair_count, first_times, table, peramb, first, sinks)
    table, a_far_up, a_far_down, a_far_two = tie((table, a_far_up, a_far_down, a_far_two))
    last = [m for a in (a_far_up, a_far_down, a_far_two) for m in (a, send(a, core=1))]
    table = both_steps(places, pair_count, last_times, table, peramb, last, sinks)
    return table[None, :, None]


def solution(mesh):
    placed = (
        P("tm", None, None, None, None),
        P("op", "tm", None, None, None),
        P("op", "tm", None, None, None),
        P("op", None),
        P("op"),
    )
    return jax.shard_map(
        body, mesh=mesh, in_specs=placed, out_specs=P("op", None, "tm", None, None), check_vma=False
    )
```

```python
import itertools

import jax
import jax.numpy as jnp
from jax import lax
from jax.experimental import pallas as pl
from jax.experimental.pallas import tpu as pltpu
from jax.sharding import PartitionSpec as P

AXES = ("tm", "op")
N = 256
SLOTS = 4
TIMES = 16
HALF = jnp.bfloat16
FULL = jnp.float32
NN = (((1,), (0,)), ((), ()))
NT = (((1,), (1,)), ((), ()))


def moves(dx=0, dy=0, core=0, z_lo=0, z_hi=0):
    def index(zl, x, c, zh, y):
        return ((zl * 4 + x % 4) * 2 + c) * 8 + zh * 4 + y % 4

    return [
        (index(zl, x, c, zh, y), index(zl ^ z_lo, x + dx, c ^ core, zh ^ z_hi, y + dy))
        for zl, x, c, zh, y in itertools.product(range(2), range(4), range(2), range(2), range(4))
    ]


def send(value, **step):
    return lax.ppermute(value, AXES, moves(**step))


def split(x):
    high = x.astype(HALF)
    return high, (x - high.astype(FULL)).astype(HALF)


def left(x):
    high, low = split(x)
    return jnp.concatenate([high, low, high], axis=1)


def right(x):
    high, low = split(x)
    return jnp.concatenate([high, high, low], axis=0)


def product(a, b, dims):
    return lax.dot_general(a, b, dims, preferred_element_type=FULL)


def x_of(peramb, source):
    pr, pi = peramb
    ar, ai = source
    (prh, prl), (pih, pil), (psh, psl), (pdh, pdl) = map(split, (pr, pi, pr + pi, pr - pi))

    def down(high, low):
        return jnp.concatenate([high, high, low], axis=1)

    def along(high, low):
        return jnp.concatenate([high, low, high], axis=1)

    k1 = product(left(ar + ai), down(prh, prl), NT)
    k2 = product(left(ar), down(psh, psl), NT)
    k3 = product(left(ai), down(pdh, pdl), NT)
    hr, hi = k1 - k3, k1 - k2
    k1 = product(along(psh, psl), right(hr), NN)
    k2 = product(along(prh, prl), right(hi - hr), NN)
    k3 = product(along(pih, pil), right(hr + hi), NN)
    return k1 - k3, k1 + k2


def trace_parts(zr, zi):
    zrt, zit = zr.T, zi.T
    re = (zr * zrt - zi * zit).reshape(32, 8, N).sum(0)
    im = (zr * zit).reshape(32, 8, N).sum(0)
    return re[:, :128] + re[:, 128:], 2.0 * (im[:, :128] + im[:, 128:])


def traces(xr, xi, ready, acc, times, step):
    x0, x1, x2 = left(xr + xi), left(xr), left(xi)
    for s in range(SLOTS):
        k1 = product(x0, ready[s, 0], NN)
        k2 = product(x1, ready[s, 1], NN)
        k3 = product(x2, ready[s, 2], NN)
        zr, zi = k1 - k3, k1 + k2
        for j in range(2):
            re, im = trace_parts(zr[j * N : (j + 1) * N], zi[j * N : (j + 1) * N])
            at = times[2 * step + j]
            acc[s, 0, at] = re
            acc[s, 1, at] = im


def prepare(sinks, ready):
    for s in range(SLOTS):
        sr, si = sinks[s, 0], sinks[s, 1]
        ready[s, 0] = right(sr)
        ready[s, 1] = right(si - sr)
        ready[s, 2] = right(si + sr)


def fetch_sinks(places, refs, sinks, sems):
    for s in range(SLOTS):
        for k, ref in enumerate(refs):

            @pl.when(places[s] == k)
            def _():
                pltpu.make_async_copy(ref, sinks.at[s], sems.at[s]).start()


def both_steps(places, count, times, before, peramb, sources, blocks):
    total = len(sources)

    def kernel(places, count_ref, times, before, p_hbm, *refs):
        sources, blocks, out = refs[:total], refs[total : total + 8], refs[total + 8]
        p_all, a_all, sinks, ready, acc, p_sems, a_sems, s_sems = refs[total + 9 :]
        step = pl.program_id(0)

        @pl.when(step == 0)
        def _():
            for k in range(total):
                pltpu.make_async_copy(p_hbm.at[times[k]], p_all.at[k], p_sems.at[k]).start()
                pltpu.make_async_copy(sources[k], a_all.at[k], a_sems.at[k]).start()
                if k == 0:
                    fetch_sinks(places, blocks, sinks, s_sems)
            acc[...] = jnp.zeros_like(acc)
            for s in range(SLOTS):
                pltpu.make_async_copy(blocks[0], sinks.at[s], s_sems.at[s]).wait()
            prepare(sinks, ready)

        xs = []
        for j in range(2):
            k = 2 * step + j
            pltpu.make_async_copy(p_hbm.at[0], p_all.at[k], p_sems.at[k]).wait()
            pltpu.make_async_copy(sources[0], a_all.at[k], a_sems.at[k]).wait()
        for j in range(2):
            k = 2 * step + j
            xs.append(x_of((p_all[k, 0], p_all[k, 1]), (a_all[k, 0], a_all[k, 1])))
        xr, xi = (jnp.concatenate([xs[0][part], xs[1][part]], axis=0) for part in range(2))
        traces(xr, xi, ready, acc, times, step)

        @pl.when(step == pl.num_programs(0) - 1)
        def _():
            slot = lax.broadcasted_iota(jnp.int32, (SLOTS, 2, TIMES), 0)
            out[...] = before[...] + jnp.where(slot < count_ref[0], acc[...].sum((3, 4)), 0.0)

    hbm = pl.BlockSpec(memory_space=pltpu.HBM)
    table = pl.BlockSpec((SLOTS, 2, TIMES), lambda g, *_: (0, 0, 0))
    return pl.pallas_call(
        kernel,
        out_shape=jax.ShapeDtypeStruct((SLOTS, 2, TIMES), FULL),
        grid_spec=pltpu.PrefetchScalarGridSpec(
            num_scalar_prefetch=3,
            grid=(total // 2,),
            in_specs=[table] + [hbm] * (1 + total + 8),
            out_specs=table,
            scratch_shapes=[
                pltpu.VMEM((total, 2, N, N), FULL),
                pltpu.VMEM((total, 2, N, N), FULL),
                pltpu.VMEM((SLOTS, 2, N, N), FULL),
                pltpu.VMEM((SLOTS, 3, 3 * N, N), HALF),
                pltpu.VMEM((SLOTS, 2, TIMES, 8, 128), FULL),
                pltpu.SemaphoreType.DMA((total,)),
                pltpu.SemaphoreType.DMA((total,)),
                pltpu.SemaphoreType.DMA((SLOTS,)),
            ],
        ),
        compiler_params=pltpu.CompilerParams(
            vmem_limit_bytes=58 << 20, dimension_semantics=("arbitrary",)
        ),
        cost_estimate=pl.CostEstimate(
            flops=total * (18 + SLOTS * 9) * 2 * N**3, bytes_accessed=16 << 20, transcendentals=0
        ),
        name="both_steps",
    )(places, count, times, before, peramb, *sources, *blocks)


def body(perambs, src_ops, sink_ops, pair_list, pair_count):
    peramb = perambs[0]
    a_own = src_ops[0, 0]
    s_own = sink_ops[0, 0]
    tm, op = lax.axis_index("tm"), lax.axis_index("op")
    x, y = (tm // 2) % 4, op % 4

    tie = lax.optimization_barrier
    s_up = send(s_own, dy=1)
    s_down = send(s_own, dy=-1)
    s_far = send(s_own, z_hi=1)
    a_up = send(a_own, dx=1)
    a_down = send(a_own, dx=-1)
    def times_of(steps):
        return jnp.stack(
            [
                (((tm // 8) ^ plane) * 4 + (x + step) % 4) * 2 + (tm % 2 ^ other)
                for plane, step in steps
                for other in range(2)
            ]
        ).astype(jnp.int32)

    b = pair_list[0]
    scalars = (
        ((b - y) % 4 + 4 * (b // 4 != op // 4)).astype(jnp.int32),
        times_of([(0, 0), (0, -1), (0, 1), (0, 2), (1, 0)]),
        times_of([(1, -1), (1, 1), (1, 2)]),
        jnp.zeros((SLOTS, 2, TIMES), FULL),
    )
    s_up, s_down, s_far, a_up, a_down, a_next, scalars = tie(
        (s_up, s_down, s_far, a_up, a_down, a_own, scalars)
    )
    places, first_times, last_times, table = scalars
    s_far_down = send(s_far, dy=-1)
    s_far_up = send(s_far, dy=1)
    s_two = send(s_up, dy=1)
    a_far = send(a_next, z_lo=1)
    a_two = send(a_next, dx=2)
    s_far_down, a_far, a_next, a_up, a_down = tie((s_far_down, a_far, a_next, a_up, a_down))
    s_far_two = send(s_far_down, dy=-1)
    beside = [send(a, core=1) for a in (a_next, a_up, a_down)]
    a_two, s_two, s_far_up, s_far_two, beside = tie((a_two, s_two, s_far_up, s_far_two, beside))
    beside += [send(a, core=1) for a in (a_two, a_far)]
    a_far_up = send(a_far, dx=1)
    a_far_down = send(a_far, dx=-1)
    a_far_two = send(a_far, dx=2)

    sinks = [s_own, s_down, s_two, s_up, s_far, s_far_down, s_far_two, s_far_up]
    first = [m for a, there in zip((a_own, a_up, a_down, a_two, a_far), beside) for m in (a, there)]
    table = both_steps(places, pair_count, first_times, table, peramb, first, sinks)
    table, a_far_up, a_far_down, a_far_two = tie((table, a_far_up, a_far_down, a_far_two))
    last = [m for a in (a_far_up, a_far_down, a_far_two) for m in (a, send(a, core=1))]
    table = both_steps(places, pair_count, last_times, table, peramb, last, sinks)
    return table[None, :, None]


def solution(mesh):
    placed = (
        P("tm", None, None, None, None),
        P("op", "tm", None, None, None),
        P("op", "tm", None, None, None),
        P("op", None),
        P("op"),
    )
    return jax.shard_map(
        body, mesh=mesh, in_specs=placed, out_specs=P("op", None, "tm", None, None), check_vma=False
    )
```

```python
import functools
import itertools

import jax
import jax.numpy as jnp
from jax import lax
from jax.experimental import pallas as pl
from jax.experimental.pallas import tpu as pltpu
from jax.sharding import PartitionSpec as P

AXES = ("tm", "op")
N = 256
SLOTS = 4
NEAR = 5
TIMES = 16
HALF = jnp.bfloat16
FULL = jnp.float32
NN = (((1,), (0,)), ((), ()))
NT = (((1,), (1,)), ((), ()))


def moves(dx=0, dy=0, core=0, z_lo=0, z_hi=0):
    def index(zl, x, c, zh, y):
        return ((zl * 4 + x % 4) * 2 + c) * 8 + zh * 4 + y % 4

    return [
        (index(zl, x, c, zh, y), index(zl ^ z_lo, x + dx, c ^ core, zh ^ z_hi, y + dy))
        for zl, x, c, zh, y in itertools.product(range(2), range(4), range(2), range(2), range(4))
    ]


def send(value, **step):
    return lax.ppermute(value, AXES, moves(**step))


def split(x):
    high = x.astype(HALF)
    return high, (x - high.astype(FULL)).astype(HALF)


def left(x):
    high, low = split(x)
    return jnp.concatenate([high, low, high], axis=1)


def right(x):
    high, low = split(x)
    return jnp.concatenate([high, high, low], axis=0)


def right_rows(x):
    high, low = split(x)
    return jnp.concatenate([high, high, low], axis=1)


def product(a, b, dims):
    return lax.dot_general(a, b, dims, preferred_element_type=FULL)


def x_kernel(count, *refs):
    peramb, source, out = refs[:count], refs[count : 2 * count], refs[-1]
    for j in range(count):
        pr, pi = peramb[j][0, 0], peramb[j][0, 1]
        ar, ai = source[j][0], source[j][1]
        k1 = product(left(ar + ai), right_rows(pr), NT)
        k2 = product(left(ar), right_rows(-pi - pr), NT)
        k3 = product(left(ai), right_rows(pr - pi), NT)
        hr, hi = k1 - k3, k1 + k2
        k1 = product(left(pr + pi), right(hr), NN)
        k2 = product(left(pr), right(hi - hr), NN)
        k3 = product(left(pi), right(hr + hi), NN)
        out[j, 0] = k1 - k3
        out[j, 1] = k1 + k2


def make_x(times, peramb, sources):
    count = len(sources)

    def body(times, *refs):
        x_kernel(count, *refs)

    def at(j):
        return pl.BlockSpec((1, 2, N, N), lambda g, times: (times[j], 0, 0, 0))

    whole = pl.BlockSpec((2, N, N), lambda g, times: (0, 0, 0))
    return pl.pallas_call(
        body,
        out_shape=jax.ShapeDtypeStruct((count, 2, N, N), FULL),
        grid_spec=pltpu.PrefetchScalarGridSpec(
            num_scalar_prefetch=1,
            grid=(1,),
            in_specs=[at(j) for j in range(count)] + [whole] * count,
            out_specs=pl.BlockSpec((count, 2, N, N), lambda g, times: (0, 0, 0, 0)),
        ),
        compiler_params=pltpu.CompilerParams(vmem_limit_bytes=20 << 20),
        cost_estimate=pl.CostEstimate(
            flops=count * 18 * 2 * N**3, bytes_accessed=count * 6 * N * N * 4, transcendentals=0
        ),
        name="make_x",
    )(times, *([peramb] * count), *sources)


def trace_parts(zr, zi):
    zrt, zit = zr.T, zi.T
    re = (zr * zrt - zi * zit).reshape(32, 8, N).sum(0)
    im = (zr * zit).reshape(32, 8, N).sum(0)
    return re[:, :128] + re[:, 128:], 2.0 * (im[:, :128] + im[:, 128:])


def z_kernel(groups, places, count_ref, times, before, *refs):
    xs = refs[: len(groups)]
    blocks = refs[len(groups) : len(groups) + 8]
    out, sinks, x_all, ready, acc, sems, x_sems = refs[len(groups) + 8 :]
    step = pl.program_id(0)

    def x_copies():
        copies, start = [], 0
        for k, size in enumerate(groups):
            copies.append(pltpu.make_async_copy(xs[k], x_all.at[pl.ds(start, size)], x_sems.at[k]))
            start += size
        return copies

    @pl.when(step == 0)
    def _():
        acc[...] = jnp.zeros_like(acc)
        for s in range(SLOTS):
            for k, ref in enumerate(blocks):

                @pl.when(places[s] == k)
                def _():
                    pltpu.make_async_copy(ref, sinks.at[s], sems.at[s]).start()

        for copy in x_copies():
            copy.start()
        for s in range(SLOTS):
            pltpu.make_async_copy(blocks[0], sinks.at[s], sems.at[s]).wait()
        for s in range(SLOTS):
            sr, si = sinks[s, 0], sinks[s, 1]
            ready[s, 0] = right(sr)
            ready[s, 1] = right(si - sr)
            ready[s, 2] = right(si + sr)
        for copy in x_copies():
            copy.wait()

    rows = 2 * N
    xr = x_all[pl.ds(2 * step, 2), 0].reshape(rows, N)
    xi = x_all[pl.ds(2 * step, 2), 1].reshape(rows, N)
    x0, x1, x2 = left(xr + xi), left(xr), left(xi)
    for s in range(SLOTS):
        k1 = product(x0, ready[s, 0], NN)
        k2 = product(x1, ready[s, 1], NN)
        k3 = product(x2, ready[s, 2], NN)
        zr, zi = k1 - k3, k1 + k2
        for j in range(2):
            re, im = trace_parts(zr[j * N : (j + 1) * N], zi[j * N : (j + 1) * N])
            at = times[2 * step + j]
            acc[s, 0, at] = re
            acc[s, 1, at] = im

    @pl.when(step == pl.num_programs(0) - 1)
    def _():
        slot = lax.broadcasted_iota(jnp.int32, (SLOTS, 2, TIMES), 0)
        out[...] = before[...] + jnp.where(slot < count_ref[0], acc[...].sum((3, 4)), 0.0)


def make_z(places, count, times, before, xs, blocks):
    groups = tuple(x.shape[0] for x in xs)
    total = sum(groups)
    anywhere = pl.BlockSpec(memory_space=pl.ANY)
    table = pl.BlockSpec((SLOTS, 2, TIMES), lambda g, *_: (0, 0, 0))
    return pl.pallas_call(
        functools.partial(z_kernel, groups),
        out_shape=jax.ShapeDtypeStruct((SLOTS, 2, TIMES), FULL),
        grid_spec=pltpu.PrefetchScalarGridSpec(
            num_scalar_prefetch=3,
            grid=(total // 2,),
            in_specs=[table] + [anywhere] * (len(xs) + 8),
            out_specs=table,
            scratch_shapes=[
                pltpu.VMEM((SLOTS, 2, N, N), FULL),
                pltpu.VMEM((total, 2, N, N), FULL),
                pltpu.VMEM((SLOTS, 3, 3 * N, N), HALF),
                pltpu.VMEM((SLOTS, 2, TIMES, 8, 128), FULL),
                pltpu.SemaphoreType.DMA((SLOTS,)),
                pltpu.SemaphoreType.DMA((len(xs),)),
            ],
        ),
        compiler_params=pltpu.CompilerParams(
            vmem_limit_bytes=20 << 20, dimension_semantics=("arbitrary",)
        ),
        cost_estimate=pl.CostEstimate(
            flops=total * SLOTS * 9 * 2 * N**3, bytes_accessed=16 << 20, transcendentals=0
        ),
        name="make_z",
    )(places, count, times, before, *xs, *blocks)


def body(perambs, src_ops, sink_ops, pair_list, pair_count):
    peramb = perambs[0]
    a_own = src_ops[0, 0]
    s_own = sink_ops[0, 0]
    tm, op = lax.axis_index("tm"), lax.axis_index("op")
    x, y = (tm // 2) % 4, op % 4

    tie = lax.optimization_barrier
    s_up = send(s_own, dy=1)
    s_down = send(s_own, dy=-1)
    s_far = send(s_own, z_hi=1)
    a_up = send(a_own, dx=1)
    a_down = send(a_own, dx=-1)
    s_up, s_down, s_far, a_up, a_down, a_next = tie((s_up, s_down, s_far, a_up, a_down, a_own))
    s_far_down = send(s_far, dy=-1)
    s_far_up = send(s_far, dy=1)
    s_two = send(s_up, dy=1)
    a_far = send(a_next, z_lo=1)
    a_two = send(a_next, dx=2)
    s_far_down, a_far, a_next = tie((s_far_down, a_far, a_next))
    s_far_two = send(s_far_down, dy=-1)
    beside = [send(a, core=1) for a in (a_next, a_up, a_down)]
    a_two, s_two, s_far_up, beside = tie((a_two, s_two, s_far_up, beside))
    beside += [send(a, core=1) for a in (a_two, a_far)]
    a_far_up = send(a_far, dx=1)
    a_far_down = send(a_far, dx=-1)
    a_far_two = send(a_far, dx=2)

    def times_of(plane, step, other):
        mine = (((tm // 8) ^ plane) * 4 + (x + step) % 4) * 2 + tm % 2
        return mine ^ other

    def pair(first, second):
        (a, *at), (b, *bt) = first, second
        times = jnp.stack([times_of(*at), times_of(*bt)]).astype(jnp.int32)
        return make_x(times, peramb, [a, b]), times

    b = pair_list[0]
    places = ((b - y) % 4 + 4 * (b // 4 != op // 4)).astype(jnp.int32)
    sinks = [s_own, s_down, s_two, s_up, s_far, s_far_down, s_far_two, s_far_up]
    early = [(a_own, 0, 0), (a_up, 0, -1), (a_down, 0, 1), (a_two, 0, 2), (a_far, 1, 0)]
    done = [pair((a, *at, 0), (there, *at, 1)) for (a, *at), there in zip(early[:NEAR], beside)]
    table = jnp.zeros((SLOTS, 2, TIMES), FULL)
    table = make_z(places, pair_count, jnp.concatenate([t for _, t in done]), table, [v for v, _ in done], sinks)
    table, a_far_up, a_far_down, a_far_two = tie((table, a_far_up, a_far_down, a_far_two))
    done = [pair((a, *at, 0), (there, *at, 1)) for (a, *at), there in zip(early[NEAR:], beside[NEAR:])]
    late = [(a_far_up, 1, -1), (a_far_down, 1, 1), (a_far_two, 1, 2)]
    there = [send(a, core=1) for a, *_ in late]
    done.append(pair((a_far_up, 1, -1, 0), (a_far_down, 1, 1, 0)))
    done.append(pair((a_far_two, 1, 2, 0), (there[0], 1, -1, 1)))
    done.append(pair((there[1], 1, 1, 1), (there[2], 1, 2, 1)))
    table = make_z(places, pair_count, jnp.concatenate([t for _, t in done]), table, [v for v, _ in done], sinks)
    return table[None, :, None]


def solution(mesh):
    placed = (
        P("tm", None, None, None, None),
        P("op", "tm", None, None, None),
        P("op", "tm", None, None, None),
        P("op", None),
        P("op"),
    )
    return jax.shard_map(
        body, mesh=mesh, in_specs=placed, out_specs=P("op", None, "tm", None, None), check_vma=False
    )
```
